32 devices in a mesh: site: 4 (over y, x), chan: 4 (over z), grp: 2 (over core).
Axes of the slice: x: 2, y: 2, z: 4, core: 2. Of those that a mesh axis runs over, the one named last changes fastest.
Arguments:
- voltages: bfloat16 [2, 8192, 3072], P(None, 'chan', ('site', 'grp')), may hold values from -6 to 6
- taps: float32 [8, 4], replicated, may hold values from -1 to 1
- sections: int32 [4, 2], replicated, may hold values from 0 to 768, as said below
- tile_list: int32 [2, 68, 2], replicated, may hold values from 0 to 15, as said below
Outputs:
- visibility: float32 [4, 4, 136, 2, 128, 128], P('site', 'chan', 'grp')
The draws below stay inside these ranges and needn't reach their ends.
Inputs may be any that keep to these rules, and one draw needn't show every extreme that they name: `sections`: the live counts sum to 2048; each is at least 128 and at most 768, one site has exactly 768; each first live column plus its count is at most 768. `tile_list`: every pair (p, q) with 0 <= p <= q < 16 stands exactly once in the whole list.
All inputs are finite; a program needn't handle non-finite values.
Results may differ from the reference program's by a relative error of at most 0.0033.
Values may be sent and summed in bfloat16 or wider, within the bound.
A program may use at most 128 MiB of HBM per device.

```python
import jax
import jax.numpy as jnp
import numpy as np
from jax import lax

NIN = 2048
CAP = 768
PANEL = 128
TAPS = 8
FB = 512
NCHAN = 4
NT = 136
TSLOT = 68
SAMPLES = 8192
N_SITE = 4


def draw_sections(key, part):
    subkeys = jax.random.split(key, 4)
    least = NIN // 16
    remain = NIN - CAP
    first_count = jax.random.randint(subkeys[0], (), max(least, remain - 2 * CAP), min(CAP, remain - 2 * least) + 1)
    second_count = jax.random.randint(subkeys[1], (), jnp.maximum(least, remain - first_count - CAP), jnp.minimum(CAP, remain - first_count - least) + 1)
    third_count = remain - first_count - second_count
    counts = jnp.stack([jnp.int32(CAP), first_count.astype(jnp.int32), second_count.astype(jnp.int32), third_count.astype(jnp.int32)])
    shuffle = jax.random.permutation(subkeys[2], 4)
    counts = counts[shuffle]
    starts = jax.random.randint(subkeys[3], (4,), 0, CAP - counts + 1)
    return jnp.stack([counts, starts.astype(jnp.int32)], axis=1).astype(jnp.int32)


def draw_tile_list(key, part):
    row_panel, col_panel = np.triu_indices(NIN // PANEL)
    pairs = jnp.stack([jnp.asarray(row_panel, jnp.int32), jnp.asarray(col_panel, jnp.int32)], axis=1)
    shuffle = jax.random.permutation(key, pairs.shape[0])
    return pairs[shuffle].reshape(-1, TSLOT, 2).astype(jnp.int32)


def block_scale(stream_key, extent, cuts, low, top_value):
    level = 1.0
    for axis_at, parts in cuts:
        heights = jax.random.uniform(jax.random.fold_in(jax.random.fold_in(stream_key, 6), axis_at), (parts,), jnp.float32, low / len(cuts), top_value / len(cuts))
        level = level * jnp.repeat(jnp.exp(heights), extent[axis_at] // parts).reshape((-1,) + (1,) * (len(extent) - 1 - axis_at))
    return level


def normal_values(own_key, extent, scale, bound, shards=(), kind=jnp.bfloat16):
    values = scale * jax.random.normal(own_key, extent, jnp.float32)
    if shards:
        values = values * block_scale(own_key, extent, shards, -0.22, 0.18)
    return jnp.clip(values, -bound, bound).astype(kind)


def setup_inputs(seed: int = 0) -> dict:
    key_list = jax.random.split(jax.random.key(seed), 5)
    voltages = normal_values(key_list[0], (2, SAMPLES, N_SITE * CAP), 1.0, 6.0, ((1, 4), (2, 8)))
    taps = normal_values(key_list[1], (TAPS, NCHAN), (TAPS * NCHAN) ** -0.5, 1.0, (), jnp.float32)
    sections = draw_sections(jax.random.fold_in(key_list[4], 71), 0)
    tile_list = draw_tile_list(jax.random.fold_in(key_list[4], 71), 0)
    return dict(voltages=voltages, taps=taps, sections=sections, tile_list=tile_list)


def dft_table(chan_count):
    positions = jnp.arange(chan_count, dtype=jnp.int32)
    products = (positions[:, None] * positions[None, :]) % chan_count
    phases = products.astype(jnp.float32) * (2.0 * jnp.pi / chan_count)
    cosine_part = jnp.cos(phases)
    sine_part = jnp.sin(phases)
    from_real = jnp.stack([cosine_part, -sine_part], axis=1)
    from_imag = jnp.stack([sine_part, cosine_part], axis=1)
    return jnp.stack([from_real, from_imag], axis=0)


def filter_frames(history, taps, transform, frames):
    tap_count = taps.shape[0]
    filtered = jnp.zeros((history.shape[0], frames, history.shape[2], history.shape[3]), jnp.float32)
    for tap_index in range(tap_count):
        first_frame = tap_count - 1 - tap_index
        filtered = filtered + taps[tap_index][None, None, :, None] * history[:, first_frame:first_frame + frames]
    spectra = jnp.einsum("qfkr,qkpm->pmfr", filtered, transform, precision=lax.Precision.HIGHEST)
    return spectra.astype(jnp.bfloat16)


def reference(voltages, taps, sections, tile_list):
    chan_count = taps.shape[1]
    frames = voltages.shape[1] // chan_count
    transform = dft_table(chan_count)
    counts = sections[:, 0]
    starts = sections[:, 1]
    offsets = jnp.cumsum(counts) - counts
    inputs = jnp.arange(NIN, dtype=jnp.int32)
    inside = (inputs[:, None] >= offsets[None, :]) & (inputs[:, None] < (offsets + counts)[None, :])
    site_ids = jnp.arange(N_SITE, dtype=jnp.int32)
    in_section = jnp.sum(jnp.where(inside, starts[None, :] + inputs[:, None] - offsets[None, :], 0), axis=1)
    owner_site = jnp.sum(jnp.where(inside, site_ids[None, :], 0), axis=1)
    columns = (owner_site * CAP + in_section).astype(jnp.int32)
    compact = jnp.take(voltages, columns, axis=2)

    def panel_spectra(panel_id):
        panel_block = lax.dynamic_slice_in_dim(compact, (panel_id * PANEL).astype(jnp.int32), PANEL, 2)
        panel_block = panel_block.reshape(2, frames, chan_count, PANEL)
        history = jnp.pad(panel_block.astype(jnp.float32), ((0, 0), (TAPS - 1, 0), (0, 0), (0, 0)))
        return filter_frames(history, taps, transform, frames)

    spectra = lax.map(panel_spectra, jnp.arange(NIN // PANEL, dtype=jnp.int32))
    slot_pairs = tile_list.reshape(-1, 2)

    def add_slot(slot_id, result):
        pair_ids = slot_pairs[slot_id]
        left_panel = spectra[pair_ids[0]].reshape(2, chan_count, N_SITE, FB, PANEL).astype(jnp.float32)
        right_panel = spectra[pair_ids[1]].reshape(2, chan_count, N_SITE, FB, PANEL).astype(jnp.float32)
        gram_block = jnp.einsum("qcbfu,rcbfv->bcqruv", left_panel, right_panel, precision=lax.Precision.HIGHEST)
        real_part = gram_block[:, :, 0, 0] + gram_block[:, :, 1, 1]
        imag_part = gram_block[:, :, 1, 0] - gram_block[:, :, 0, 1]
        tile_value = jnp.stack([real_part, imag_part], axis=2) / FB
        return lax.dynamic_update_slice_in_dim(result, tile_value[:, :, None], slot_id.astype(jnp.int32), 2)

    result = jnp.zeros((N_SITE, chan_count, NT, 2, PANEL, PANEL), jnp.float32)
    return lax.fori_loop(0, NT, add_slot, result)
```

```python
import functools

import jax
import jax.numpy as jnp
import numpy as np
from jax import lax
from jax.experimental import pallas as pl
from jax.experimental.pallas import tpu as pltpu
from jax.sharding import PartitionSpec as P

NIN = 2048
PANEL = 128
CHUNKS = 4
MESH = pl.DeviceIdType.MESH


def filter_constants(tap_count, chan_count, frames):
    width = (tap_count + frames) * chan_count
    sample = np.arange(width)
    position = sample % chan_count
    pos = np.stack([sample // chan_count, position]).astype(np.int32)
    chan = np.arange(chan_count)
    phase = (chan[:, None] * position[None, :] % chan_count) * (2.0 * np.pi / chan_count)
    cosine, sine = np.cos(phase), np.sin(phase)
    table = np.stack([np.stack([cosine, sine], 1), np.stack([-sine, cosine], 1)], 1)
    return pos, table.reshape(chan_count * 4, width).astype(np.float32)


def exchange_kernel(
    dims, x_ref, taps_ref, pos_ref, table_ref, out_ref,
    spec_ref, land_ref, halo_ref, weight_ref,
    halo_sem, z_send, z_recv, x_send, x_recv, g_send, g_recv,
):
    tap_count, chan_count, frames, sub, n_site, n_chan, n_grp = dims
    cols = x_ref.shape[2]
    ratio = n_chan // n_site
    chunk = frames // CHUNKS
    width = (tap_count + sub) * chan_count
    back = tap_count * chan_count
    site, chan, grp = lax.axis_index("site"), lax.axis_index("chan"), lax.axis_index("grp")

    def offset(me, step, total):
        return lax.rem(me + step, total)

    barrier = pltpu.get_barrier_semaphore()
    partners = 0
    for name, me, total in (("chan", chan, n_chan), ("site", site, n_site), ("grp", grp, n_grp)):
        for step in range(1, total):
            pl.semaphore_signal(
                barrier, inc=1, device_id={name: offset(me, step, total)}, device_id_type=MESH
            )
            partners += 1
    pl.semaphore_wait(barrier, partners)

    def halo_copy():
        return pltpu.make_async_remote_copy(
            src_ref=x_ref.at[:, pl.ds(x_ref.shape[1] - back, back), :],
            dst_ref=halo_ref,
            send_sem=halo_sem.at[0],
            recv_sem=halo_sem.at[1],
            device_id={"chan": offset(chan, 1, n_chan)},
            device_id_type=MESH,
        )

    @pl.when(chan < n_chan - 1)
    def _():
        halo_copy().start()

    frame_of = pos_ref[0:1, :]
    place_of = pos_ref[1:2, :]
    lag = lax.broadcasted_iota(jnp.int32, (sub, width), 0) + tap_count - frame_of
    base = jnp.zeros((sub, width), jnp.float32)
    for t in range(tap_count):
        row = jnp.zeros((1, width), jnp.float32)
        for k in range(chan_count):
            row = jnp.where(place_of == k, taps_ref[t, k], row)
        base = jnp.where(lag == t, row, base)
    for m in range(chan_count):
        for q in range(2):
            for p in range(2):
                index = (m * 2 + q) * 2 + p
                full = base * table_ref[index : index + 1, :]
                high = full.astype(jnp.bfloat16)
                low = (full - high.astype(jnp.float32)).astype(jnp.bfloat16)
                rows = pl.ds((m * 2 + q) * sub, sub)
                weight_ref[p, 0, rows, :] = high
                weight_ref[p, 1, rows, :] = low

    def put_spectra(first_frame, window):
        total = None
        for p in range(2):
            for part in range(2):
                term = jnp.dot(
                    weight_ref[p, part], window[p], preferred_element_type=jnp.float32
                )
                total = term if total is None else total + term
        total = total.astype(jnp.bfloat16).reshape(chan_count, 2, sub, cols)
        spec_ref[:, :, pl.ds(pl.multiple_of(first_frame, 16), sub), :] = total

    def filter_chunk(k):
        per_chunk = chunk // sub
        if k == 0:
            @pl.when(chan == 0)
            def _():
                halo_ref[...] = jnp.zeros_like(halo_ref)

            @pl.when(chan > 0)
            def _():
                halo_copy().wait_recv()

            put_spectra(
                0,
                [
                    jnp.concatenate([halo_ref[p], x_ref[p, : sub * chan_count, :]], axis=0)
                    for p in range(2)
                ],
            )

        def body(u, carry):
            first = (k * per_chunk + u) * sub
            start = pl.multiple_of(first * chan_count - back, 16)
            put_spectra(first, [x_ref[p, pl.ds(start, width), :] for p in range(2)])
            return carry

        lax.fori_loop(1 if k == 0 else 0, per_chunk, body, 0)

    def span(k):
        return pl.ds(k * chunk, chunk)

    def z_copy(step, k):
        there = offset(chan, step, n_chan)
        return pltpu.make_async_remote_copy(
            src_ref=spec_ref.at[there, :, span(k), :],
            dst_ref=land_ref.at[chan, :, span(k), :],
            send_sem=z_send.at[step, k],
            recv_sem=z_recv.at[step, k],
            device_id={"chan": there},
            device_id_type=MESH,
        )

    def slot(section, sub_block, k):
        start = pl.multiple_of(sub_block * frames + k * chunk, 16)
        return out_ref.at[section, :, pl.ds(start, chunk), :]

    def forward(step, k, own, begin):
        block = lax.rem(chan + n_chan - step, n_chan)
        owner = block // ratio
        sub_block = lax.rem(block, ratio)
        source = spec_ref.at[chan, :, span(k), :] if own else land_ref.at[block, :, span(k), :]
        target = slot(site * n_grp + grp, sub_block, k)

        @pl.when(owner != site)
        def _():
            copy = pltpu.make_async_remote_copy(
                src_ref=source,
                dst_ref=target,
                send_sem=x_send.at[step, k],
                recv_sem=x_recv.at[site, sub_block, k],
                device_id={"site": owner},
                device_id_type=MESH,
            )
            if begin:
                copy.start()
            else:
                copy.wait_send()

        if begin:
            @pl.when(owner == site)
            def _():
                pltpu.make_async_copy(source, target, x_recv.at[site, sub_block, k]).start()

    def cross(from_site, sub_block, k):
        mine = slot(from_site * n_grp + grp, sub_block, k)
        return [
            pltpu.make_async_remote_copy(
                src_ref=mine,
                dst_ref=mine,
                send_sem=g_send.at[step - 1, from_site, sub_block, k],
                recv_sem=g_recv.at[step - 1, from_site, sub_block, k],
                device_id={"grp": offset(grp, step, n_grp)},
                device_id_type=MESH,
            )
            for step in range(1, n_grp)
        ]

    def each(body, *sizes):
        low, high = sizes
        def run(index, carry):
            body(index)
            return carry
        lax.fori_loop(low, high, run, 0, unroll=high - low <= 4)

    def over_blocks(body):
        def run(index):
            body(lax.rem(index // ratio + site, n_site), lax.rem(index, ratio))
        each(run, 0, n_site * ratio)

    order = list(range(1, CHUNKS)) + [0]
    for k in order:
        filter_chunk(k)
        each(lambda step: z_copy(step, k).start(), 1, n_chan)
        forward(0, k, True, True)

    def hand_over(k):
        def run(from_site, sub_block):
            here = slot(from_site * n_grp + grp, sub_block, k)
            pltpu.make_async_copy(here, here, x_recv.at[from_site, sub_block, k]).wait()
            for copy in cross(from_site, sub_block, k):
                copy.start()
        over_blocks(run)

    for place, k in enumerate(order):
        def relay(step):
            z_copy(step, k).wait_recv()
            forward(step, k, False, True)
        each(relay, 1, n_chan)
        if place:
            hand_over(order[place - 1])
    hand_over(order[-1])

    @pl.when(chan < n_chan - 1)
    def _():
        halo_copy().wait_send()

    for k in order:
        each(lambda step: z_copy(step, k).wait_send(), 1, n_chan)
        forward(0, k, True, False)
        each(lambda step: forward(step, k, False, False), 1, n_chan)

        def finish(from_site, sub_block):
            for copy in cross(from_site, sub_block, k):
                copy.wait_send()
                copy.wait_recv()
        over_blocks(finish)


def exchange(voltages, taps):
    tap_count, chan_count = taps.shape
    n_site, n_chan, n_grp = (lax.axis_size(a) for a in ("site", "chan", "grp"))
    assert n_chan == chan_count
    frames = voltages.shape[1] // chan_count
    cols = voltages.shape[2]
    sub = min(frames // CHUNKS, max(16, 128 // chan_count))
    width = (tap_count + sub) * chan_count
    ratio = n_chan // n_site
    pos, table = filter_constants(tap_count, chan_count, sub)
    dims = (tap_count, chan_count, frames, sub, n_site, n_chan, n_grp)
    vmem = pl.BlockSpec(memory_space=pltpu.VMEM)
    dma = pltpu.SemaphoreType.DMA
    return pl.pallas_call(
        functools.partial(exchange_kernel, dims),
        out_shape=jax.ShapeDtypeStruct((n_site * n_grp, 2, ratio * frames, cols), jnp.bfloat16),
        in_specs=[vmem, pl.BlockSpec(memory_space=pltpu.SMEM), vmem, vmem],
        out_specs=pl.BlockSpec(memory_space=pl.ANY),
        scratch_shapes=[
            pltpu.VMEM((chan_count, 2, frames, cols), jnp.bfloat16),
            pltpu.VMEM((n_chan, 2, frames, cols), jnp.bfloat16),
            pltpu.VMEM((2, tap_count * chan_count, cols), jnp.bfloat16),
            pltpu.VMEM((2, 2, chan_count * 2 * sub, width), jnp.bfloat16),
            dma((2,)),
            dma((n_chan, CHUNKS)),
            dma((n_chan, CHUNKS)),
            dma((n_chan, CHUNKS)),
            dma((n_site, ratio, CHUNKS)),
            dma((n_grp - 1, n_site, ratio, CHUNKS)),
            dma((n_grp - 1, n_site, ratio, CHUNKS)),
        ],
        compiler_params=pltpu.CompilerParams(
            collective_id=0, has_side_effects=True, vmem_limit_bytes=48 * 1024 * 1024
        ),
    )(voltages, taps, jnp.asarray(pos), jnp.asarray(table))


def tiles_kernel(dims, sections_ref, pairs_ref, spec_ref, out_ref, left_ref, right_ref):
    n_site, n_grp, per_step = dims
    frames, cols = spec_ref.shape[2:]
    per_half = cols // PANEL
    blocks = n_grp * per_half
    step = pl.program_id(0)

    @pl.when(step == 0)
    def _():
        counts = [sections_ref[s, 0] for s in range(n_site)]
        offsets = [jnp.int32(0)]
        for s in range(n_site - 1):
            offsets.append(offsets[-1] + counts[s])
        source = lax.broadcasted_iota(jnp.int32, (2 * PANEL, PANEL), 0)
        column = lax.broadcasted_iota(jnp.int32, (2 * PANEL, PANEL), 1)

        def one_panel(panel, carry):
            first = panel * PANEL

            def site_of(index):
                return sum((index >= offsets[s]).astype(jnp.int32) for s in range(1, n_site))

            low_site, high_site = site_of(first), site_of(first + PANEL - 1)
            windows, selects = [], []
            for which, owner in enumerate((low_site, high_site)):
                offset = sum(jnp.where(s < owner, counts[s], 0) for s in range(n_site - 1))
                count, start = sections_ref[owner, 0], sections_ref[owner, 1]
                begin = start - offset + first
                block = jnp.clip(begin >> (PANEL.bit_length() - 1), 0, blocks - 2)
                shift = begin - block * PANEL
                low = offset - first
                high = low + count
                if which:
                    high = jnp.where(low_site == high_site, low, high)
                hit = (source == column + shift) & (column >= low) & (column < high)
                selects.append(hit.astype(jnp.float32).astype(jnp.bfloat16))
                for extra in range(2):
                    here = block + extra
                    half = here // per_half
                    lane = pl.multiple_of((here - half * per_half) * PANEL, PANEL)
                    part = spec_ref[owner * n_grp + half, :, :, pl.ds(lane, PANEL)]
                    windows.append(part.reshape(2 * frames, PANEL))
            packed = jnp.dot(
                jnp.concatenate(windows, axis=1),
                jnp.concatenate(selects, axis=0),
                preferred_element_type=jnp.float32,
            )
            value = packed.astype(jnp.bfloat16)
            right_ref[panel, :, :PANEL] = value
            right_ref[panel, :frames, PANEL:] = -value[frames:]
            right_ref[panel, frames:, PANEL:] = value[:frames]
            left_ref[panel] = packed.T.astype(jnp.bfloat16)
            return carry

        lax.fori_loop(0, NIN // PANEL, one_panel, 0)

    slots = pl.num_programs(0) * per_step
    base = (lax.axis_index("grp") * slots + step * per_step) * 2
    for i in range(per_step):
        tile = jnp.dot(
            left_ref[pairs_ref[base + 2 * i]],
            right_ref[pairs_ref[base + 2 * i + 1]],
            preferred_element_type=jnp.float32,
        ) * (1.0 / frames)
        out_ref[0, 0, i, 0] = tile[:, :PANEL]
        out_ref[0, 0, i, 1] = tile[:, PANEL:]


def correlate(spectra, sections, tile_list):
    n_site, n_grp = lax.axis_size("site"), lax.axis_size("grp")
    slots = tile_list.shape[1]
    per_step = max(d for d in range(1, 5) if slots % d == 0)
    frames = spectra.shape[2]
    panels = NIN // PANEL
    return pl.pallas_call(
        functools.partial(tiles_kernel, (n_site, n_grp, per_step)),
        out_shape=jax.ShapeDtypeStruct((1, 1, slots, 2, PANEL, PANEL), jnp.float32),
        grid_spec=pltpu.PrefetchScalarGridSpec(
            num_scalar_prefetch=2,
            grid=(slots // per_step,),
            in_specs=[pl.BlockSpec(memory_space=pltpu.VMEM)],
            out_specs=pl.BlockSpec(
                (1, 1, per_step, 2, PANEL, PANEL), lambda i, *_: (0, 0, i, 0, 0, 0)
            ),
            scratch_shapes=[
                pltpu.VMEM((panels, PANEL, 2 * frames), jnp.bfloat16),
                pltpu.VMEM((panels, 2 * frames, 2 * PANEL), jnp.bfloat16),
            ],
        ),
        compiler_params=pltpu.CompilerParams(vmem_limit_bytes=48 * 1024 * 1024),
    )(sections, tile_list.reshape(-1), spectra)


def per_device(voltages, taps, sections, tile_list):
    return correlate(exchange(voltages, taps), sections, tile_list)


def solution(mesh):
    in_specs = (P(None, "chan", ("site", "grp")), P(), P(), P())
    out_specs = P("site", "chan", "grp", None, None, None)
    return jax.shard_map(
        per_device, mesh=mesh, in_specs=in_specs, out_specs=out_specs, check_vma=False
    )
```

```python
import functools

import jax
import jax.numpy as jnp
import numpy as np
from jax import lax
from jax.experimental import pallas as pl
from jax.experimental.pallas import tpu as pltpu
from jax.sharding import PartitionSpec as P

NIN = 2048
PANEL = 128
MOST_CHUNKS = 4
MESH = pl.DeviceIdType.MESH


def chunk_total(frames):
    return min(MOST_CHUNKS, frames // 16)


def pack_panels(sections_ref, load, left_ref, right_ref, n_site, blocks):
    rows = left_ref.shape[2]
    frames = rows // 2
    counts = [sections_ref[0, s] for s in range(n_site)]
    starts = [sections_ref[1, s] for s in range(n_site)]
    offsets = [jnp.int32(0)]
    for s in range(n_site - 1):
        offsets.append(offsets[-1] + counts[s])
    source = lax.broadcasted_iota(jnp.int32, (2 * PANEL, PANEL), 0)
    column = lax.broadcasted_iota(jnp.int32, (2 * PANEL, PANEL), 1)

    def pick(values, owner):
        result = values[0]
        for s in range(1, n_site):
            result = jnp.where(owner == s, values[s], result)
        return result

    def one_panel(panel, carry):
        first = panel * PANEL

        def site_of(index):
            return sum((index >= offsets[s]).astype(jnp.int32) for s in range(1, n_site))

        low_site, high_site = site_of(first), site_of(first + PANEL - 1)
        windows, selects = [], []
        for which, owner in enumerate((low_site, high_site)):
            offset, count, start = (pick(v, owner) for v in (offsets, counts, starts))
            begin = start - offset + first
            block = jnp.clip(begin >> (PANEL.bit_length() - 1), 0, blocks - 2)
            shift = begin - block * PANEL
            low = offset - first
            high = low + count
            if which:
                high = jnp.where(low_site == high_site, low, high)
            hit = (source == column + shift) & (column >= low) & (column < high)
            selects.append(hit.astype(jnp.float32).astype(jnp.bfloat16))
            for extra in range(2):
                windows.append(load(owner, block + extra).reshape(rows, PANEL))
        packed = jnp.dot(
            jnp.concatenate(windows, axis=1),
            jnp.concatenate(selects, axis=0),
            preferred_element_type=jnp.float32,
        )
        value = packed.astype(jnp.bfloat16)
        right_ref[panel, :, :PANEL] = value
        right_ref[panel, :frames, PANEL:] = -value[frames:]
        right_ref[panel, frames:, PANEL:] = value[:frames]
        left_ref[panel] = packed.T.astype(jnp.bfloat16)
        return carry

    lax.fori_loop(0, NIN // PANEL, one_panel, 0)


def column_block(ref, n_grp):
    per_half = ref.shape[3] // PANEL

    def load(owner, block):
        half = block // per_half
        lane = pl.multiple_of((block - half * per_half) * PANEL, PANEL)
        return ref[owner * n_grp + half, :, :, pl.ds(lane, PANEL)]

    return load


def exchange_kernel(
    dims, volts_ref, taps_ref, sections_hbm, last_ref, sums_ref,
    x_ref, spec_ref, land_ref, halo_ref, weight_ref, sections_ref,
    total_ref, select_ref, flat_ref, left_ref, right_ref,
    load_sem, halo_sem, z_send, z_recv, x_send, x_recv, g_send, g_recv, *block_refs,
):
    tap_count, chan_count, frames, sub, n_site, n_chan, n_grp = dims
    cols = x_ref.shape[2]
    ratio = n_chan // n_site
    chunks = chunk_total(frames)
    chunk = frames // chunks
    order = list(range(1, chunks)) + [0]
    width = (tap_count + sub) * chan_count
    back = tap_count * chan_count
    site, chan, grp = lax.axis_index("site"), lax.axis_index("chan"), lax.axis_index("grp")

    def offset(me, step, total):
        return lax.rem(me + step, total)

    loads = [
        pltpu.make_async_copy(volts_ref, x_ref, load_sem.at[0]),
        pltpu.make_async_copy(sections_hbm, sections_ref, load_sem.at[1]),
    ]
    for copy in loads:
        copy.start()

    barrier = pltpu.get_barrier_semaphore()
    partners = 0
    for name, me, total in (("chan", chan, n_chan), ("site", site, n_site), ("grp", grp, n_grp)):
        for step in range(1, total):
            pl.semaphore_signal(
                barrier, inc=1, device_id={name: offset(me, step, total)}, device_id_type=MESH
            )
            partners += 1

    sample = lax.broadcasted_iota(jnp.int32, (1, width), 1)
    place_of = lax.rem(sample, chan_count)
    lag = lax.broadcasted_iota(jnp.int32, (sub, width), 0) + tap_count - sample // chan_count
    base = jnp.zeros((sub, width), jnp.float32)
    for t in range(tap_count):
        row = jnp.zeros((1, width), jnp.float32)
        for k in range(chan_count):
            row = jnp.where(place_of == k, taps_ref[k : k + 1, t : t + 1], row)
        base = jnp.where(lag == t, row, base)
    for m in range(chan_count):
        cosine = jnp.zeros((1, width), jnp.float32)
        sine = jnp.zeros((1, width), jnp.float32)
        for k in range(chan_count):
            angle = (m * k % chan_count) * (2.0 * np.pi / chan_count)
            cosine = jnp.where(place_of == k, float(np.cos(angle)), cosine)
            sine = jnp.where(place_of == k, float(np.sin(angle)), sine)
        for q, p, factor in ((0, 0, cosine), (0, 1, sine), (1, 0, -sine), (1, 1, cosine)):
            full = base * factor
            high = full.astype(jnp.bfloat16)
            low = (full - high.astype(jnp.float32)).astype(jnp.bfloat16)
            rows = pl.ds((m * 2 + q) * sub, sub)
            weight_ref[p, 0, rows, :] = high
            weight_ref[p, 1, rows, :] = low

    loads[0].wait()
    pl.semaphore_wait(barrier, partners)

    def halo_copy():
        return pltpu.make_async_remote_copy(
            src_ref=x_ref.at[:, pl.ds(x_ref.shape[1] - back, back), :],
            dst_ref=halo_ref,
            send_sem=halo_sem.at[0],
            recv_sem=halo_sem.at[1],
            device_id={"chan": offset(chan, 1, n_chan)},
            device_id_type=MESH,
        )

    @pl.when(chan < n_chan - 1)
    def _():
        halo_copy().start()

    def put_spectra(first_frame, window):
        total = None
        for p in range(2):
            for part in range(2):
                term = jnp.dot(
                    weight_ref[p, part], window[p], preferred_element_type=jnp.float32
                )
                total = term if total is None else total + term
        total = total.astype(jnp.bfloat16).reshape(chan_count, 2, sub, cols)
        spec_ref[:, :, pl.ds(pl.multiple_of(first_frame, 16), sub), :] = total

    def filter_chunk(k):
        per_chunk = chunk // sub
        if k == 0:
            @pl.when(chan == 0)
            def _():
                halo_ref[...] = jnp.zeros_like(halo_ref)

            @pl.when(chan > 0)
            def _():
                halo_copy().wait_recv()

            put_spectra(
                0,
                [
                    jnp.concatenate([halo_ref[p], x_ref[p, : sub * chan_count, :]], axis=0)
                    for p in range(2)
                ],
            )

        def body(u, carry):
            first = (k * per_chunk + u) * sub
            start = pl.multiple_of(first * chan_count - back, 16)
            put_spectra(first, [x_ref[p, pl.ds(start, width), :] for p in range(2)])
            return carry

        lax.fori_loop(1 if k == 0 else 0, per_chunk, body, 0)

    def span(k):
        return pl.ds(k * chunk, chunk)

    def z_copy(step, k):
        there = offset(chan, step, n_chan)
        return pltpu.make_async_remote_copy(
            src_ref=spec_ref.at[there, :, span(k), :],
            dst_ref=land_ref.at[chan, :, span(k), :],
            send_sem=z_send.at[step, k],
            recv_sem=z_recv.at[step, k],
            device_id={"chan": there},
            device_id_type=MESH,
        )

    def slot(section, sub_block, k):
        start = pl.multiple_of(sub_block * chunk, 16)
        block_ref = last_ref if k == order[-1] else block_refs[order.index(k)]
        return block_ref.at[section, :, pl.ds(start, chunk), :]

    def forward(step, k, own, begin):
        block = lax.rem(chan + n_chan - step, n_chan)
        owner = block // ratio
        sub_block = lax.rem(block, ratio)
        source = spec_ref.at[chan, :, span(k), :] if own else land_ref.at[block, :, span(k), :]
        target = slot(site * n_grp + grp, sub_block, k)

        @pl.when(owner != site)
        def _():
            copy = pltpu.make_async_remote_copy(
                src_ref=source,
                dst_ref=target,
                send_sem=x_send.at[step, k],
                recv_sem=x_recv.at[site, sub_block, k],
                device_id={"site": owner},
                device_id_type=MESH,
            )
            if begin:
                copy.start()
            else:
                copy.wait_send()

        if begin:
            @pl.when(owner == site)
            def _():
                pltpu.make_async_copy(source, target, x_recv.at[site, sub_block, k]).start()

    def cross(from_site, sub_block, k):
        mine = slot(from_site * n_grp + grp, sub_block, k)
        return [
            pltpu.make_async_remote_copy(
                src_ref=mine,
                dst_ref=mine,
                send_sem=g_send.at[step - 1, from_site, sub_block, k],
                recv_sem=g_recv.at[step - 1, from_site, sub_block, k],
                device_id={"grp": offset(grp, step, n_grp)},
                device_id_type=MESH,
            )
            for step in range(1, n_grp)
        ]

    def each(body, *sizes):
        low, high = sizes
        def run(index, carry):
            body(index)
            return carry
        lax.fori_loop(low, high, run, 0, unroll=high - low <= 4)

    def over_blocks(body):
        def run(index):
            body(lax.rem(index // ratio + site, n_site), lax.rem(index, ratio))
        each(run, 0, n_site * ratio)

    for k in order:
        filter_chunk(k)
        each(lambda step: z_copy(step, k).start(), 1, n_chan)
        forward(0, k, True, True)

    def hand_over(k):
        def run(from_site, sub_block):
            here = slot(from_site * n_grp + grp, sub_block, k)
            pltpu.make_async_copy(here, here, x_recv.at[from_site, sub_block, k]).wait()
            for copy in cross(from_site, sub_block, k):
                copy.start()
        over_blocks(run)

    def take_over(k):
        def run(from_site, sub_block):
            for copy in cross(from_site, sub_block, k):
                copy.wait_recv()
        over_blocks(run)

    loads[1].wait()

    live = 0
    section = n_grp * cols
    for which in range(n_site):
        count, start = sections_ref[0, which], sections_ref[1, which]

        def fill(part, carry, which=which, count=count, start=start, live=live):
            row = lax.broadcasted_iota(jnp.int32, (PANEL, 1), 0) + part * PANEL - start
            place = jnp.where((row >= 0) & (row < count), row + live, -1)
            column = lax.broadcasted_iota(jnp.int32, (PANEL, NIN), 1)
            first = pl.multiple_of(which * section + part * PANEL, PANEL)
            select_ref[pl.ds(first, PANEL), :] = jnp.where(column == place, 1.0, 0.0).astype(
                jnp.bfloat16
            )
            return carry

        lax.fori_loop(0, section // PANEL, fill, 0)
        live = live + count

    def add_tiles(place):
        rows = flat_ref.shape[0]
        half = rows // 2
        for part in range(n_site * n_grp):
            flat_ref[:, part * cols : (part + 1) * cols] = block_refs[place][part].reshape(
                rows, cols
            )

        def one_pair(pair, carry):
            columns = pl.ds(pl.multiple_of(pair * 2 * PANEL, PANEL), 2 * PANEL)
            packed = jnp.dot(
                flat_ref[...], select_ref[:, columns], preferred_element_type=jnp.float32
            )
            left_ref[columns, :] = packed.T.astype(jnp.bfloat16)
            value = packed.astype(jnp.bfloat16)
            for i in range(2):
                piece = value[:, i * PANEL : (i + 1) * PANEL]
                right_ref[2 * pair + i, :, :PANEL] = piece
                right_ref[2 * pair + i, :half, PANEL:] = -piece[half:]
                right_ref[2 * pair + i, half:, PANEL:] = piece[:half]
            return carry

        lax.fori_loop(0, NIN // (2 * PANEL), one_pair, 0)
        for q in range(NIN // PANEL):
            first = q * (q + 1) // 2
            tiles = jnp.dot(
                left_ref[: (q + 1) * PANEL, :], right_ref[q], preferred_element_type=jnp.float32
            ).reshape(q + 1, PANEL, 2 * PANEL)
            if place:
                tiles = total_ref[first : first + q + 1] + tiles
            total_ref[first : first + q + 1] = tiles

    for place, k in enumerate(order):
        def relay(step):
            z_copy(step, k).wait_recv()
            forward(step, k, False, True)
        each(relay, 1, n_chan)
        if place:
            hand_over(order[place - 1])
            take_over(order[place - 1])
            add_tiles(place - 1)
    store = pltpu.make_async_copy(total_ref, sums_ref, load_sem.at[0])
    store.start()
    hand_over(order[-1])
    take_over(order[-1])
    store.wait()

    @pl.when(chan < n_chan - 1)
    def _():
        halo_copy().wait_send()

    for k in order:
        each(lambda step: z_copy(step, k).wait_send(), 1, n_chan)
        forward(0, k, True, False)
        each(lambda step: forward(step, k, False, False), 1, n_chan)

        def finish(from_site, sub_block):
            for copy in cross(from_site, sub_block, k):
                copy.wait_send()
        over_blocks(finish)


def exchange(voltages, taps, sections):
    chan_count, tap_count = taps.shape
    n_site, n_chan, n_grp = (lax.axis_size(a) for a in ("site", "chan", "grp"))
    assert n_chan == chan_count
    frames = voltages.shape[1] // chan_count
    cols = voltages.shape[2]
    chunks = chunk_total(frames)
    chunk = frames // chunks
    sub = min(chunk, max(16, 128 // chan_count))
    width = (tap_count + sub) * chan_count
    ratio = n_chan // n_site
    panels = NIN // PANEL
    tiles = panels * (panels + 1) // 2
    block = (n_site * n_grp, 2, ratio * chunk, cols)
    dims = (tap_count, chan_count, frames, sub, n_site, n_chan, n_grp)
    anywhere = pl.BlockSpec(memory_space=pl.ANY)
    dma = pltpu.SemaphoreType.DMA
    return pl.pallas_call(
        functools.partial(exchange_kernel, dims),
        out_shape=[
            jax.ShapeDtypeStruct(block, jnp.bfloat16),
            jax.ShapeDtypeStruct((tiles, PANEL, 2 * PANEL), jnp.float32),
        ],
        in_specs=[anywhere, pl.BlockSpec(memory_space=pltpu.VMEM), anywhere],
        out_specs=[anywhere, anywhere],
        scratch_shapes=[
            pltpu.VMEM(voltages.shape, jnp.bfloat16),
            pltpu.VMEM((chan_count, 2, frames, cols), jnp.bfloat16),
            pltpu.VMEM((n_chan, 2, frames, cols), jnp.bfloat16),
            pltpu.VMEM((2, tap_count * chan_count, cols), jnp.bfloat16),
            pltpu.VMEM((2, 2, chan_count * 2 * sub, width), jnp.bfloat16),
            pltpu.SMEM(sections.shape, jnp.int32),
            pltpu.VMEM((tiles, PANEL, 2 * PANEL), jnp.float32),
            pltpu.VMEM((n_site * n_grp * cols, NIN), jnp.bfloat16),
            pltpu.VMEM((2 * ratio * chunk, n_site * n_grp * cols), jnp.bfloat16),
            pltpu.VMEM((NIN, 2 * ratio * chunk), jnp.bfloat16),
            pltpu.VMEM((panels, 2 * ratio * chunk, 2 * PANEL), jnp.bfloat16),
            dma((2,)),
            dma((2,)),
            dma((n_chan, chunks)),
            dma((n_chan, chunks)),
            dma((n_chan, chunks)),
            dma((n_site, ratio, chunks)),
            dma((n_grp - 1, n_site, ratio, chunks)),
            dma((n_grp - 1, n_site, ratio, chunks)),
        ]
        + [pltpu.VMEM(block, jnp.bfloat16) for _ in range(chunks - 1)],
        compiler_params=pltpu.CompilerParams(
            collective_id=0, has_side_effects=True, vmem_limit_bytes=60 * 1024 * 1024
        ),
    )(voltages, taps, sections)


def tiles_kernel(
    dims, block_ref, sections_hbm, pairs_hbm, sums_hbm, out_ref,
    left_ref, right_ref, sections_ref, pairs_ref, sums_ref, load_sem, sums_sem,
):
    n_site, n_grp, per_step, scale = dims
    step = pl.program_id(0)
    grp = lax.axis_index("grp")

    def pair(at, i):
        index = at * per_step + i
        return pairs_ref[grp, 0, index], pairs_ref[grp, 1, index]

    def fetch(at, i):
        p, q = pair(at, i)
        held = lax.rem(at, 2)
        return pltpu.make_async_copy(
            sums_hbm.at[(q * (q + 1) >> 1) + p], sums_ref.at[held, i], sums_sem.at[held, i]
        )

    @pl.when(step == 0)
    def _():
        loads = [
            pltpu.make_async_copy(sections_hbm, sections_ref, load_sem.at[0]),
            pltpu.make_async_copy(pairs_hbm, pairs_ref, load_sem.at[1]),
        ]
        for copy in loads:
            copy.start()
        for copy in loads:
            copy.wait()
        for i in range(per_step):
            fetch(step, i).start()
        blocks = n_grp * block_ref.shape[3] // PANEL
        pack_panels(
            sections_ref, column_block(block_ref, n_grp), left_ref, right_ref, n_site, blocks
        )

    @pl.when(step + 1 < pl.num_programs(0))
    def _():
        for i in range(per_step):
            fetch(step + 1, i).start()

    for i in range(per_step):
        fetch(step, i).wait()
    for i in range(per_step):
        p, q = pair(step, i)
        tile = jnp.dot(left_ref[p], right_ref[q], preferred_element_type=jnp.float32)
        tile = (sums_ref[lax.rem(step, 2), i] + tile) * scale
        out_ref[0, 0, i, 0] = tile[:, :PANEL]
        out_ref[0, 0, i, 1] = tile[:, PANEL:]


def correlate(block, sums, sections, tile_list, frames):
    n_site, n_grp = lax.axis_size("site"), lax.axis_size("grp")
    slots = tile_list.shape[2]
    per_step = max(d for d in range(1, 5) if slots % d == 0)
    rows = 2 * block.shape[2]
    panels = NIN // PANEL
    anywhere = pl.BlockSpec(memory_space=pl.ANY)
    return pl.pallas_call(
        functools.partial(tiles_kernel, (n_site, n_grp, per_step, 1.0 / frames)),
        out_shape=jax.ShapeDtypeStruct((1, 1, slots, 2, PANEL, PANEL), jnp.float32),
        grid=(slots // per_step,),
        in_specs=[
            pl.BlockSpec(memory_space=pltpu.VMEM),
            anywhere,
            anywhere,
            anywhere,
        ],
        out_specs=pl.BlockSpec(
            (1, 1, per_step, 2, PANEL, PANEL), lambda i: (0, 0, i, 0, 0, 0)
        ),
        scratch_shapes=[
            pltpu.VMEM((panels, PANEL, rows), jnp.bfloat16),
            pltpu.VMEM((panels, rows, 2 * PANEL), jnp.bfloat16),
            pltpu.SMEM(sections.shape, jnp.int32),
            pltpu.SMEM(tile_list.shape, jnp.int32),
            pltpu.VMEM((2, per_step, PANEL, 2 * PANEL), jnp.float32),
            pltpu.SemaphoreType.DMA((2,)),
            pltpu.SemaphoreType.DMA((2, per_step)),
        ],
        compiler_params=pltpu.CompilerParams(vmem_limit_bytes=60 * 1024 * 1024),
    )(block, sections, tile_list, sums)


def per_device(voltages, taps, sections, tile_list):
    taps, sections = taps.T, sections.T
    tile_list = jnp.swapaxes(tile_list, 1, 2)
    block, sums = exchange(voltages, taps, sections)
    block_frames = voltages.shape[1] // taps.shape[0] * (
        lax.axis_size("chan") // lax.axis_size("site")
    )
    return correlate(block, sums, sections, tile_list, block_frames)


def solution(mesh):
    in_specs = (P(None, "chan", ("site", "grp")), P(), P(), P())
    out_specs = P("site", "chan", "grp", None, None, None)
    return jax.shard_map(
        per_device, mesh=mesh, in_specs=in_specs, out_specs=out_specs, check_vma=False
    )
```

```python
import functools

import jax
import jax.numpy as jnp
import numpy as np
from jax import lax
from jax.experimental import pallas as pl
from jax.experimental.pallas import tpu as pltpu
from jax.sharding import PartitionSpec as P

NIN = 2048
PANEL = 128
MOST_CHUNKS = 8
MESH = pl.DeviceIdType.MESH


def exchange_kernel(
    dims, volts_ref, taps_ref, out_ref,
    x_ref, spec_ref, land_ref, halo_ref, weight_ref,
    load_sem, halo_sem, z_send, z_recv, x_send, x_recv, g_send, g_recv,
):
    tap_count, chan_count, frames, sub, n_site, n_chan, n_grp = dims
    cols = x_ref.shape[2]
    ratio = n_chan // n_site
    chunks = min(MOST_CHUNKS, frames // 16)
    chunk = frames // chunks
    width = (tap_count + sub) * chan_count
    back = tap_count * chan_count
    site, chan, grp = lax.axis_index("site"), lax.axis_index("chan"), lax.axis_index("grp")

    def offset(me, step, total):
        return lax.rem(me + step, total)

    load = pltpu.make_async_copy(volts_ref, x_ref, load_sem.at[0])
    load.start()
    barrier = pltpu.get_barrier_semaphore()
    partners = 0
    for name, me, total in (("chan", chan, n_chan), ("site", site, n_site), ("grp", grp, n_grp)):
        for step in range(1, total):
            pl.semaphore_signal(
                barrier, inc=1, device_id={name: offset(me, step, total)}, device_id_type=MESH
            )
            partners += 1

    sample = lax.broadcasted_iota(jnp.int32, (1, width), 1)
    place_of = lax.rem(sample, chan_count)
    lag = lax.broadcasted_iota(jnp.int32, (sub, width), 0) + tap_count - sample // chan_count
    base = jnp.zeros((sub, width), jnp.float32)
    for t in range(tap_count):
        row = jnp.zeros((1, width), jnp.float32)
        for k in range(chan_count):
            row = jnp.where(place_of == k, taps_ref[k : k + 1, t : t + 1], row)
        base = jnp.where(lag == t, row, base)
    for m in range(chan_count):
        cosine = jnp.zeros((1, width), jnp.float32)
        sine = jnp.zeros((1, width), jnp.float32)
        for k in range(chan_count):
            angle = (m * k % chan_count) * (2.0 * np.pi / chan_count)
            cosine = jnp.where(place_of == k, float(np.cos(angle)), cosine)
            sine = jnp.where(place_of == k, float(np.sin(angle)), sine)
        for q, p, factor in ((0, 0, cosine), (0, 1, sine), (1, 0, -sine), (1, 1, cosine)):
            full = base * factor
            high = full.astype(jnp.bfloat16)
            low = (full - high.astype(jnp.float32)).astype(jnp.bfloat16)
            rows = pl.ds((m * 2 + q) * sub, sub)
            weight_ref[p, 0, rows, :] = high
            weight_ref[p, 1, rows, :] = low

    load.wait()
    pl.semaphore_wait(barrier, partners)

    def halo_copy():
        return pltpu.make_async_remote_copy(
            src_ref=x_ref.at[:, pl.ds(x_ref.shape[1] - back, back), :],
            dst_ref=halo_ref,
            send_sem=halo_sem.at[0],
            recv_sem=halo_sem.at[1],
            device_id={"chan": offset(chan, 1, n_chan)},
            device_id_type=MESH,
        )

    @pl.when(chan < n_chan - 1)
    def _():
        halo_copy().start()

    def put_spectra(first_frame, window):
        total = None
        for p in range(2):
            for part in range(2):
                term = jnp.dot(
                    weight_ref[p, part], window[p], preferred_element_type=jnp.float32
                )
                total = term if total is None else total + term
        total = total.astype(jnp.bfloat16).reshape(chan_count, 2, sub, cols)
        spec_ref[:, :, pl.ds(pl.multiple_of(first_frame, 16), sub), :] = total

    def filter_chunk(k):
        per_chunk = chunk // sub
        if k == 0:
            @pl.when(chan == 0)
            def _():
                halo_ref[...] = jnp.zeros_like(halo_ref)

            @pl.when(chan > 0)
            def _():
                halo_copy().wait_recv()

            put_spectra(
                0,
                [
                    jnp.concatenate([halo_ref[p], x_ref[p, : sub * chan_count, :]], axis=0)
                    for p in range(2)
                ],
            )

        def body(u, carry):
            first = (k * per_chunk + u) * sub
            start = pl.multiple_of(first * chan_count - back, 16)
            put_spectra(first, [x_ref[p, pl.ds(start, width), :] for p in range(2)])
            return carry

        lax.fori_loop(1 if k == 0 else 0, per_chunk, body, 0)

    def span(k):
        return pl.ds(k * chunk, chunk)

    def z_copy(step, k):
        there = offset(chan, step, n_chan)
        return pltpu.make_async_remote_copy(
            src_ref=spec_ref.at[there, :, span(k), :],
            dst_ref=land_ref.at[chan, :, span(k), :],
            send_sem=z_send.at[step, k],
            recv_sem=z_recv.at[step, k],
            device_id={"chan": there},
            device_id_type=MESH,
        )

    def slot(section, sub_block, k):
        start = pl.multiple_of(sub_block * frames + k * chunk, 16)
        return out_ref.at[section, :, pl.ds(start, chunk), :]

    def forward(step, k, own, begin):
        block = lax.rem(chan + n_chan - step, n_chan)
        owner = block // ratio
        sub_block = lax.rem(block, ratio)
        source = spec_ref.at[chan, :, span(k), :] if own else land_ref.at[block, :, span(k), :]
        target = slot(site * n_grp + grp, sub_block, k)

        @pl.when(owner != site)
        def _():
            copy = pltpu.make_async_remote_copy(
                src_ref=source,
                dst_ref=target,
                send_sem=x_send.at[step, k],
                recv_sem=x_recv.at[site, sub_block, k],
                device_id={"site": owner},
                device_id_type=MESH,
            )
            if begin:
                copy.start()
            else:
                copy.wait_send()

        if begin:
            @pl.when(owner == site)
            def _():
                pltpu.make_async_copy(source, target, x_recv.at[site, sub_block, k]).start()

    def cross(from_site, sub_block, k):
        mine = slot(from_site * n_grp + grp, sub_block, k)
        return [
            pltpu.make_async_remote_copy(
                src_ref=mine,
                dst_ref=mine,
                send_sem=g_send.at[step - 1, from_site, sub_block, k],
                recv_sem=g_recv.at[step - 1, from_site, sub_block, k],
                device_id={"grp": offset(grp, step, n_grp)},
                device_id_type=MESH,
            )
            for step in range(1, n_grp)
        ]

    def each(body, *sizes):
        low, high = sizes
        def run(index, carry):
            body(index)
            return carry
        lax.fori_loop(low, high, run, 0, unroll=high - low <= 4)

    def over_blocks(body):
        def run(index):
            body(lax.rem(index // ratio + site, n_site), lax.rem(index, ratio))
        each(run, 0, n_site * ratio)

    order = list(range(1, chunks)) + [0]
    for k in order:
        filter_chunk(k)
        each(lambda step: z_copy(step, k).start(), 1, n_chan)
        forward(0, k, True, True)

    def hand_over(k):
        def run(from_site, sub_block):
            here = slot(from_site * n_grp + grp, sub_block, k)
            pltpu.make_async_copy(here, here, x_recv.at[from_site, sub_block, k]).wait()
            for copy in cross(from_site, sub_block, k):
                copy.start()
        over_blocks(run)

    for place, k in enumerate(order):
        def relay(step):
            z_copy(step, k).wait_recv()
            forward(step, k, False, True)
        each(relay, 1, n_chan)
        if place:
            hand_over(order[place - 1])
    hand_over(order[-1])

    @pl.when(chan < n_chan - 1)
    def _():
        halo_copy().wait_send()

    for k in order:
        each(lambda step: z_copy(step, k).wait_send(), 1, n_chan)
        forward(0, k, True, False)
        each(lambda step: forward(step, k, False, False), 1, n_chan)

        def finish(from_site, sub_block):
            for copy in cross(from_site, sub_block, k):
                copy.wait_send()
                copy.wait_recv()
        over_blocks(finish)


def exchange(voltages, taps):
    chan_count, tap_count = taps.shape
    n_site, n_chan, n_grp = (lax.axis_size(a) for a in ("site", "chan", "grp"))
    assert n_chan == chan_count
    frames = voltages.shape[1] // chan_count
    cols = voltages.shape[2]
    chunks = min(MOST_CHUNKS, frames // 16)
    sub = min(frames // chunks, max(16, 128 // chan_count))
    width = (tap_count + sub) * chan_count
    ratio = n_chan // n_site
    dims = (tap_count, chan_count, frames, sub, n_site, n_chan, n_grp)
    vmem = pl.BlockSpec(memory_space=pltpu.VMEM)
    dma = pltpu.SemaphoreType.DMA
    return pl.pallas_call(
        functools.partial(exchange_kernel, dims),
        out_shape=jax.ShapeDtypeStruct((n_site * n_grp, 2, ratio * frames, cols), jnp.bfloat16),
        in_specs=[pl.BlockSpec(memory_space=pl.ANY), vmem],
        out_specs=pl.BlockSpec(memory_space=pl.ANY),
        scratch_shapes=[
            pltpu.VMEM(voltages.shape, jnp.bfloat16),
            pltpu.VMEM((chan_count, 2, frames, cols), jnp.bfloat16),
            pltpu.VMEM((n_chan, 2, frames, cols), jnp.bfloat16),
            pltpu.VMEM((2, tap_count * chan_count, cols), jnp.bfloat16),
            pltpu.VMEM((2, 2, chan_count * 2 * sub, width), jnp.bfloat16),
            dma((1,)),
            dma((2,)),
            dma((n_chan, chunks)),
            dma((n_chan, chunks)),
            dma((n_chan, chunks)),
            dma((n_site, ratio, chunks)),
            dma((n_grp - 1, n_site, ratio, chunks)),
            dma((n_grp - 1, n_site, ratio, chunks)),
        ],
        compiler_params=pltpu.CompilerParams(
            collective_id=0, has_side_effects=True, vmem_limit_bytes=60 * 1024 * 1024
        ),
    )(voltages, taps)


def tiles_kernel(
    dims, sections_hbm, pairs_hbm, spec_ref, out_ref,
    left_ref, right_ref, sections_ref, pairs_ref, load_sem,
):
    n_site, n_grp, per_step = dims
    frames, cols = spec_ref.shape[2:]
    per_half = cols // PANEL
    blocks = n_grp * per_half
    step = pl.program_id(0)

    @pl.when(step == 0)
    def _():
        loads = [
            pltpu.make_async_copy(sections_hbm, sections_ref, load_sem.at[0]),
            pltpu.make_async_copy(pairs_hbm, pairs_ref, load_sem.at[1]),
        ]
        for copy in loads:
            copy.start()
        for copy in loads:
            copy.wait()
        counts = [sections_ref[0, s] for s in range(n_site)]
        offsets = [jnp.int32(0)]
        for s in range(n_site - 1):
            offsets.append(offsets[-1] + counts[s])
        source = lax.broadcasted_iota(jnp.int32, (2 * PANEL, PANEL), 0)
        column = lax.broadcasted_iota(jnp.int32, (2 * PANEL, PANEL), 1)

        def one_panel(panel, carry):
            first = panel * PANEL

            def site_of(index):
                return sum((index >= offsets[s]).astype(jnp.int32) for s in range(1, n_site))

            low_site, high_site = site_of(first), site_of(first + PANEL - 1)
            windows, selects = [], []
            for which, owner in enumerate((low_site, high_site)):
                offset = sum(jnp.where(s < owner, counts[s], 0) for s in range(n_site - 1))
                count, start = sections_ref[0, owner], sections_ref[1, owner]
                begin = start - offset + first
                block = jnp.clip(begin >> (PANEL.bit_length() - 1), 0, blocks - 2)
                shift = begin - block * PANEL
                low = offset - first
                high = low + count
                if which:
                    high = jnp.where(low_site == high_site, low, high)
                hit = (source == column + shift) & (column >= low) & (column < high)
                selects.append(hit.astype(jnp.float32).astype(jnp.bfloat16))
                for extra in range(2):
                    here = block + extra
                    half = here // per_half
                    lane = pl.multiple_of((here - half * per_half) * PANEL, PANEL)
                    part = spec_ref[owner * n_grp + half, :, :, pl.ds(lane, PANEL)]
                    windows.append(part.reshape(2 * frames, PANEL))
            packed = jnp.dot(
                jnp.concatenate(windows, axis=1),
                jnp.concatenate(selects, axis=0),
                preferred_element_type=jnp.float32,
            )
            value = packed.astype(jnp.bfloat16)
            right_ref[panel, :, :PANEL] = value
            right_ref[panel, :frames, PANEL:] = -value[frames:]
            right_ref[panel, frames:, PANEL:] = value[:frames]
            left_ref[panel] = packed.T.astype(jnp.bfloat16)
            return carry

        lax.fori_loop(0, NIN // PANEL, one_panel, 0, unroll=2)

    grp = lax.axis_index("grp")
    base = step * per_step
    for i in range(per_step):
        tile = jnp.dot(
            left_ref[pairs_ref[grp, 0, base + i]],
            right_ref[pairs_ref[grp, 1, base + i]],
            preferred_element_type=jnp.float32,
        ) * (1.0 / frames)
        out_ref[0, 0, i, 0] = tile[:, :PANEL]
        out_ref[0, 0, i, 1] = tile[:, PANEL:]


def correlate(spectra, sections, tile_list):
    n_site, n_grp = lax.axis_size("site"), lax.axis_size("grp")
    slots = tile_list.shape[2]
    per_step = max(d for d in range(1, 18) if slots % d == 0)
    frames = spectra.shape[2]
    panels = NIN // PANEL
    return pl.pallas_call(
        functools.partial(tiles_kernel, (n_site, n_grp, per_step)),
        out_shape=jax.ShapeDtypeStruct((1, 1, slots, 2, PANEL, PANEL), jnp.float32),
        grid=(slots // per_step,),
        in_specs=[
            pl.BlockSpec(memory_space=pl.ANY),
            pl.BlockSpec(memory_space=pl.ANY),
            pl.BlockSpec(memory_space=pltpu.VMEM),
        ],
        out_specs=pl.BlockSpec(
            (1, 1, per_step, 2, PANEL, PANEL), lambda i: (0, 0, i, 0, 0, 0)
        ),
        scratch_shapes=[
            pltpu.VMEM((panels, PANEL, 2 * frames), jnp.bfloat16),
            pltpu.VMEM((panels, 2 * frames, 2 * PANEL), jnp.bfloat16),
            pltpu.SMEM(sections.shape, jnp.int32),
            pltpu.SMEM(tile_list.shape, jnp.int32),
            pltpu.SemaphoreType.DMA((2,)),
        ],
        compiler_params=pltpu.CompilerParams(vmem_limit_bytes=60 * 1024 * 1024),
    )(sections, tile_list, spectra)


def per_device(voltages, taps, sections, tile_list):
    tile_list = jnp.swapaxes(tile_list, 1, 2)
    return correlate(exchange(voltages, taps.T), sections.T, tile_list)


def solution(mesh):
    in_specs = (P(None, "chan", ("site", "grp")), P(), P(), P())
    out_specs = P("site", "chan", "grp", None, None, None)
    return jax.shard_map(
        per_device, mesh=mesh, in_specs=in_specs, out_specs=out_specs, check_vma=False
    )
```
